32 devices in a mesh: members: 2 (over y), cards: 4 (over z), sub: 2 (over x), rep: 2 (over core).
Axes of the slice: x: 2, y: 2, z: 4, core: 2. Of those that a mesh axis runs over, the one named last changes fastest.
Arguments:
- spectra: float32 [36, 32, 2, 8192], P('rep', None, 'sub', ('members', 'cards')), parts along dimension 3, may hold values from 0.02 to 0.6
- deal_slot: int32 [2, 8192], P('sub', 'members'), parts along dimension 1, may hold values from 0 to 4095, each once within a row
- sea_mask: int32 [32, 512], P('sub', 'members'), parts along dimension 1, may hold values 0 or 1
- ice_class: int32 [2, 8192], P('sub', ('members', 'cards')), parts along dimension 1, may hold values from 0 to 3
- brine: float32 [2, 8192], P('sub', ('members', 'cards')), parts along dimension 1, may hold values from 0.02 to 0.3
- wind_rate: float32 [2, 8192], P('sub', ('members', 'cards')), parts along dimension 1, may hold values from 0 to 0.6
- wind_dir: float32 [2, 8192], P('sub', ('members', 'cards')), parts along dimension 1, may hold values from -3.140625 to 3.140625
- ice_table: float32 [4, 32], replicated, may hold values from 0.05 to 1.5
Outputs:
- spectra_out: float32 [36, 32, 2, 8192], P('rep', None, 'sub', ('members', 'cards')), parts along dimension 3
The draws below stay inside these ranges and needn't reach their ends.
There are 2 independent parts, one for each index of `members`. The reference program is written for one: setup_inputs(seed, part) draws one part's arguments, and reference() takes and returns one part's arrays. A program takes and returns all parts, laid end to end along the dimension named above; an argument that names none is the same for every part. Nothing has to cross between parts.
Inputs may be any that keep to these rules, and one draw needn't show every extreme that they name: `deal_slot`: each row is a permutation of the slots of its row block.
All inputs are finite; a program needn't handle non-finite values. No bound on the sum of `sea_mask` on one device may be relied on, other than what follows from the above.
Results may differ from the reference program's by a relative error of at most 0.000098.
Values sent between devices are 32-bit elements; how exact they have to be, the bound alone decides.
A program may use at most 64 MiB of HBM per device.

```python
import math
import jax
import jax.numpy as jnp

ND = 36
NF = 32
NCLASS = 4
NSTEP = 2
NC = 256
NR = 32
CELLS_BLK = 4096
N_SUB = 2


def set_ends(array, key, smallest, high):
    spot = [jax.random.randint(jax.random.fold_in(key, axis), (), 0, length) for axis, length in enumerate(array.shape)]
    widest = array.shape.index(max(array.shape))
    neighbour = spot[:widest] + [(spot[widest] + 1) % array.shape[widest]] + spot[widest + 1:]
    return array.at[tuple(spot)].set(smallest).at[tuple(neighbour)].set(high)


def block_scale(stream_key, extent, split, smallest, top_value):
    level = 1.0
    for dim, shards_of in split:
        steps = jax.random.uniform(jax.random.fold_in(jax.random.fold_in(stream_key, 6), dim), (shards_of,), jnp.float32, smallest / len(split), top_value / len(split))
        level = level * jnp.repeat(jnp.exp(steps), extent[dim] // shards_of).reshape((-1,) + (1,) * (len(extent) - 1 - dim))
    return level


def setup_inputs(seed: int = 0, part: int = 0) -> dict:
    splits = jax.random.split(jax.random.key(seed), 9)
    part_keys = jax.random.split(jax.random.fold_in(splits[8], part), 9)
    return {
        "spectra": jnp.clip(jnp.exp(math.log(0.6) - 3.4011974 * jax.random.uniform(part_keys[0], (ND, NF, N_SUB, CELLS_BLK), jnp.float32) ** block_scale(part_keys[0], (ND, NF, N_SUB, CELLS_BLK), ((0, 2), (2, 2), (3, 4)), -0.2, 0.2)), 0.02, 0.6),
        "deal_slot": jax.vmap(lambda own: jax.random.permutation(own, CELLS_BLK))(jax.random.split(part_keys[1], N_SUB)).reshape((N_SUB, CELLS_BLK)).astype(jnp.int32),
        "sea_mask": set_ends((jax.random.randint(part_keys[2], (NR, NC), 0, 8) < 7).astype(jnp.int32), jax.random.fold_in(part_keys[2], 1), 0, 1),
        "ice_class": set_ends(jax.random.randint(part_keys[3], (N_SUB, CELLS_BLK), 0, NCLASS), jax.random.fold_in(part_keys[3], 1), 0, NCLASS - 1).astype(jnp.int32),
        "brine": jnp.clip(0.02 + 0.28 * jax.random.uniform(part_keys[4], (N_SUB, CELLS_BLK), jnp.float32) ** block_scale(part_keys[4], (N_SUB, CELLS_BLK), ((0, 2), (1, 4)), -0.2, 0.2), 0.02, 0.3),
        "wind_rate": jnp.clip(0.6 * jax.random.uniform(part_keys[5], (N_SUB, CELLS_BLK), jnp.float32) ** block_scale(part_keys[5], (N_SUB, CELLS_BLK), ((0, 2), (1, 4)), -0.2, 0.2), 0.0, 0.6),
        "wind_dir": jnp.clip(jax.random.uniform(part_keys[6], (N_SUB, CELLS_BLK), jnp.float32, -3.140625, 3.140625), -3.140625, 3.140625),
        "ice_table": jnp.clip(jnp.exp(jax.random.uniform(splits[7], (NCLASS, NF), jnp.float32, math.log(0.05), math.log(1.5))), 0.05, 1.5),
    }


F0 = 0.035
GROWTH = 1.1
CNL = 0.25
COURANT = 0.6

def freq_up(x):
    return jnp.concatenate([x[:, 1:], jnp.zeros_like(x[:, :1])], axis=1)

def freq_down(x):
    return jnp.concatenate([jnp.zeros_like(x[:, :1]), x[:, :-1]], axis=1)

def reference(spectra, deal_slot, sea_mask, ice_class, brine, wind_rate, wind_dir, ice_table):
    theta = 2.0 * jnp.pi * jnp.arange(ND, dtype=jnp.float32) / ND
    freq = F0 * GROWTH ** jnp.arange(NF, dtype=jnp.float32)
    speed = COURANT * (freq[0] / freq)
    nux = (jnp.cos(theta)[:, None] * speed[None, :])[:, :, None, None]
    nuy = (jnp.sin(theta)[:, None] * speed[None, :])[:, :, None, None]
    beta = wind_rate[None, None] * jnp.maximum(jnp.cos(theta[:, None, None, None] - wind_dir[None, None]), 0.0) * (freq / freq[-1])[None, :, None, None]
    rate = jnp.moveaxis(ice_table[ice_class], -1, 0) * jnp.sqrt(brine / 0.1)[None]
    growth = jnp.exp(beta - rate[None])
    blocks = jnp.arange(N_SUB, dtype=jnp.int32)[:, None]
    grid_index = (blocks * CELLS_BLK + deal_slot).reshape(-1)
    cell_of = jnp.zeros((N_SUB, CELLS_BLK), jnp.int32).at[blocks, deal_slot].set(jnp.arange(CELLS_BLK, dtype=jnp.int32)[None, :])
    dealt_index = (blocks * CELLS_BLK + cell_of).reshape(-1)
    maskf = sea_mask.astype(jnp.float32)
    energy = spectra
    for step in range(NSTEP):
        plus_d = jnp.roll(energy, -1, axis=0)
        minus_d = jnp.roll(energy, 1, axis=0)
        pone = freq_up(plus_d)
        mone = freq_down(minus_d)
        ptwo = freq_up(minus_d)
        mtwo = freq_down(plus_d)
        nonlin = CNL * (energy * energy * (pone + mone + ptwo + mtwo) - 2.0 * energy * (pone * mone + ptwo * mtwo))
        energy = energy * growth + nonlin
        grid = jnp.take(energy.reshape(ND, NF, N_SUB * CELLS_BLK), grid_index, axis=2).reshape(ND, NF, NR, NC)
        left = jnp.pad(grid, ((0, 0), (0, 0), (0, 0), (1, 0)))[..., :-1]
        right = jnp.pad(grid, ((0, 0), (0, 0), (0, 0), (0, 1)))[..., 1:]
        below = jnp.pad(grid, ((0, 0), (0, 0), (1, 0), (0, 0)))[:, :, :-1, :]
        above = jnp.pad(grid, ((0, 0), (0, 0), (0, 1), (0, 0)))[:, :, 1:, :]
        moved = grid - jnp.maximum(nux, 0.0) * (grid - left) - jnp.minimum(nux, 0.0) * (right - grid) - jnp.maximum(nuy, 0.0) * (grid - below) - jnp.minimum(nuy, 0.0) * (above - grid)
        moved = moved * maskf[None, None]
        energy = jnp.take(moved.reshape(ND, NF, N_SUB * CELLS_BLK), dealt_index, axis=2).reshape(ND, NF, N_SUB, CELLS_BLK)
    return energy
```

```python
import jax
import jax.numpy as jnp
from jax import lax
from jax.sharding import PartitionSpec as P

NSTEP = 2


F0 = 0.035
GROWTH = 1.1
CNL = 0.25
COURANT = 0.6


def extended(block, sides, width, periodic):
    for axis, dim in sides:
        count = lax.axis_size(axis)
        forward = [(i, i + 1) for i in range(count - 1)]
        if periodic:
            forward.append((count - 1, 0))
        backward = [(target, source) for source, target in forward]
        low = lax.ppermute(
            lax.slice_in_dim(block, block.shape[dim] - width, None, axis=dim), axis, forward
        )
        high = lax.ppermute(lax.slice_in_dim(block, 0, width, axis=dim), axis, backward)
        block = jnp.concatenate([low, block, high], axis=dim)
    return block


def freq_up(x):
    return jnp.concatenate([x[:, 1:], jnp.zeros_like(x[:, :1])], axis=1)


def freq_down(x):
    return jnp.concatenate([jnp.zeros_like(x[:, :1]), x[:, :-1]], axis=1)


def dir_pair(energy):
    framed = extended(energy, (("rep", 0),), 1, True)
    return (framed[2:], framed[:-2])


def nonlinear(energy, pone, mone, ptwo, mtwo):
    return CNL * (
        energy * energy * (pone + mone + ptwo + mtwo) - 2.0 * energy * (pone * mone + ptwo * mtwo)
    )


def edges(block, axis, dim, width):
    count = lax.axis_size(axis)
    forward = [(i, i + 1) for i in range(count - 1)]
    backward = [(i + 1, i) for i in range(count - 1)]
    size = block.shape[dim]
    low = lax.ppermute(lax.slice_in_dim(block, size - width, None, axis=dim), axis, forward)
    high = lax.ppermute(lax.slice_in_dim(block, 0, width, axis=dim), axis, backward)
    return low, high


def propagate(grid, nux, nuy, maskf):
    framed = extended(grid, (("sub", 2),), 1, False)
    below = framed[:, :, :-2, :]
    above = framed[:, :, 2:, :]
    left = jnp.pad(grid, ((0, 0), (0, 0), (0, 0), (1, 0)))[..., :-1]
    right = jnp.pad(grid, ((0, 0), (0, 0), (0, 0), (0, 1)))[..., 1:]
    moved = (
        grid
        - jnp.maximum(nux, 0.0) * (grid - left)
        - jnp.minimum(nux, 0.0) * (right - grid)
        - jnp.maximum(nuy, 0.0) * (grid - below)
        - jnp.minimum(nuy, 0.0) * (above - grid)
    )
    return moved * maskf


def growth_of(theta, freq_ratio, table, classes, brine, wind_rate, wind_dir):
    beta = (
        wind_rate[None, None, :]
        * jnp.maximum(jnp.cos(theta[:, None, None] - wind_dir[None, None, :]), 0.0)
        * freq_ratio[None, :, None]
    )
    rate = jnp.zeros((table.shape[1], classes.shape[0]), jnp.float32)
    for k in range(table.shape[0]):
        rate = jnp.where(classes[None, :] == k, table[k][:, None], rate)
    rate = rate * jnp.sqrt(brine / 0.1)[None, :]
    return jnp.exp(beta - rate[None])


def shards(spectra, deal_slot, sea_mask, ice_class, brine, wind_rate, wind_dir, ice_table):
    dir_count, freq_count, _, point_count = spectra.shape
    card_count = lax.axis_size("cards")
    card = lax.axis_index("cards")
    rep_count = lax.axis_size("rep")
    rep_index = lax.axis_index("rep")
    own = freq_count // card_count
    all_dirs_count = dir_count * rep_count
    theta_all = 2.0 * jnp.pi * jnp.arange(all_dirs_count, dtype=jnp.float32) / all_dirs_count
    theta = lax.dynamic_slice_in_dim(theta_all, rep_index * dir_count, dir_count, 0)
    freq = F0 * GROWTH ** jnp.arange(freq_count, dtype=jnp.float32)
    speed = lax.dynamic_slice_in_dim(COURANT * (freq[0] / freq), card * own, own, 0)
    ratio = freq / freq[-1]
    slot_of = deal_slot[0]
    block_cells = slot_of.shape[0]
    cell_of = (
        jnp.zeros((block_cells,), jnp.int32)
        .at[slot_of]
        .set(jnp.arange(block_cells, dtype=jnp.int32))
    )
    rows_here, columns = sea_mask.shape
    maskf = sea_mask.astype(jnp.float32)[None, None]
    energy = spectra[:, :, 0, :]
    nux = (jnp.cos(theta)[:, None] * speed[None, :])[:, :, None, None]
    nuy = (jnp.sin(theta)[:, None] * speed[None, :])[:, :, None, None]

    growth = growth_of(
        theta, ratio, ice_table, ice_class[0], brine[0], wind_rate[0], wind_dir[0]
    )
    points = jnp.stack([ice_class[0].astype(jnp.float32), brine[0], wind_rate[0], wind_dir[0]])
    points = lax.all_gather(points, "cards", axis=1, tiled=True)
    points = jnp.take(points, slot_of, axis=1)
    growth_own = growth_of(
        theta,
        lax.dynamic_slice_in_dim(ratio, card * own, own, 0),
        lax.dynamic_slice_in_dim(ice_table, card * own, own, 1),
        points[0].astype(jnp.int32), points[1], points[2], points[3],
    )

    plus_d, minus_d = dir_pair(energy)
    nonlin = nonlinear(
        energy, freq_up(plus_d), freq_down(minus_d), freq_up(minus_d), freq_down(plus_d)
    )
    energy = energy * growth + nonlin
    energy = lax.all_to_all(energy, "cards", split_axis=1, concat_axis=2, tiled=True)
    grid = jnp.take(energy, slot_of, axis=2).reshape(dir_count, own, rows_here, columns)
    for step in range(NSTEP):
        if step > 0:
            flat = grid.reshape(dir_count, own, block_cells)
            low, high = edges(flat, "cards", 1, 1)
            tall = extended(jnp.concatenate([low, flat, high], axis=1), (("rep", 0),), 1, True)
            plus_d, minus_d = tall[2:], tall[:-2]
            nonlin = nonlinear(
                flat, plus_d[:, 2:], minus_d[:, :-2], minus_d[:, 2:], plus_d[:, :-2]
            )
            grid = (flat * growth_own + nonlin).reshape(dir_count, own, rows_here, columns)
        grid = propagate(grid, nux, nuy, maskf)
    done = jnp.take(grid.reshape(dir_count, own, block_cells), cell_of, axis=2)
    energy = lax.all_to_all(done, "cards", split_axis=2, concat_axis=1, tiled=True)
    return energy[:, :, None, :]


def solution(mesh):
    placed = (
        P("rep", None, "sub", ("members", "cards")),
        P("sub", "members"),
        P("sub", "members"),
        P("sub", ("members", "cards")),
        P("sub", ("members", "cards")),
        P("sub", ("members", "cards")),
        P("sub", ("members", "cards")),
        P(),
    )
    return jax.shard_map(
        shards,
        mesh=mesh,
        in_specs=placed,
        out_specs=P("rep", None, "sub", ("members", "cards")),
        check_vma=False,
    )
```

```python
import functools

import jax
import jax.numpy as jnp
from jax import lax
from jax.experimental import pallas as pl
from jax.experimental.pallas import tpu as pltpu
from jax.sharding import PartitionSpec as P

F0 = 0.035
GROWTH = 1.1
CNL = 0.25
COURANT = 0.6
MESH = pl.DeviceIdType.MESH


def nonlinear(energy, pone, mone, ptwo, mtwo):
    return CNL * (
        energy * energy * (pone + mone + ptwo + mtwo) - 2.0 * energy * (pone * mone + ptwo * mtwo)
    )


def rate_of(cols, classes, root, class_count):
    rate = jnp.zeros((cols.shape[0], classes.shape[1]), jnp.float32)
    for k in range(class_count):
        rate = jnp.where(jnp.abs(classes - k) < 0.5, cols[:, k : k + 1], rate)
    return rate * root


def kernel(
    sizes, x, slot, marks, pts, ang, fall, fown, out,
    halo, send, recv, precv, lhs, acc, g, flo, fhi, elo, ehi, rows1, rows2,
    rate1, rate2, mv, lhs2, sback, rback, ssem, rsem,
):
    dirs, freqs, points, n, own, ns, nrep, classes, cols = sizes
    cells = n * points
    comp = dirs * own
    pad = send.shape[1]
    me = lax.axis_index("cards")
    sub = lax.axis_index("sub")
    rep = lax.axis_index("rep")
    rep_next, rep_prev = lax.rem(rep + 1, nrep), lax.rem(rep + nrep - 1, nrep)
    sub_next, sub_prev = lax.rem(sub + 1, ns), lax.rem(sub + ns - 1, ns)

    barrier = pltpu.get_barrier_semaphore()

    def greet(o, carry):
        pl.semaphore_signal(
            barrier, inc=1, device_id={"cards": lax.rem(me + o, n)}, device_id_type=MESH
        )
        return carry

    lax.fori_loop(1, n, greet, 0)
    for name, other in (("rep", rep_next), ("rep", rep_prev), ("sub", sub_next), ("sub", sub_prev)):
        pl.semaphore_signal(barrier, inc=1, device_id={name: other}, device_id_type=MESH)
    pl.semaphore_wait(barrier, n - 1 + 4)

    def copy(src, dst, sem, name, other):
        return pltpu.make_async_remote_copy(
            src_ref=src, dst_ref=dst, send_sem=ssem.at[sem], recv_sem=rsem.at[sem],
            device_id={name: other}, device_id_type=MESH,
        )

    REP1, SUB1, SUB2, FRQ, REP2, PAR = 0, 2, 4, 6, 8, 14
    AIN = PAR + n
    AOUT = AIN + n

    rep1 = [
        copy(x.at[0], halo.at[1], REP1, "rep", rep_prev),
        copy(x.at[dirs - 1], halo.at[0], REP1 + 1, "rep", rep_next),
    ]
    for c in rep1:
        c.start()

    def par_copy(o):
        return copy(pts, precv.at[me], PAR + o, "cards", lax.rem(me + o, n))

    def in_copy(o):
        to = lax.rem(me + o, n)
        return copy(send.at[to], recv.at[me], AIN + o, "cards", to)

    def out_copy(o):
        to = lax.rem(me + o, n)
        return copy(sback.at[to], rback.at[me], AOUT + o, "cards", to)

    def each(first, last, body):
        def step(i, carry):
            body(i)
            return carry

        lax.fori_loop(first, last, step, 0)

    each(1, n, lambda o: par_copy(o).start())

    rate1[...] = rate_of(fall, pts[2:3, :], pts[3:4, :], classes)
    lane = min(256, points)

    def source1(d, plus, minus):
        def tile(t):
            at = pl.ds(pl.multiple_of(t * lane, lane), lane)
            row = lax.broadcasted_iota(jnp.int32, (freqs, lane), 0)

            def up(v):
                return jnp.where(row == freqs - 1, 0.0, pltpu.roll(v, freqs - 1, 0))

            def down(v):
                return jnp.where(row == 0, 0.0, pltpu.roll(v, 1, 0))

            e, p, m = x[d, :, at], plus(at), minus(at)
            beta = jnp.maximum(ang[0, d] * pts[0:1, at] + ang[1, d] * pts[1:2, at], 0.0)
            grow = jnp.exp(beta * fall[:, classes : classes + 1] - rate1[:, at])
            s = e * grow + nonlinear(e, up(p), down(m), up(m), down(p))
            for k in range(n):
                send[k, pl.ds(pl.multiple_of(d * own, own), own), at] = s[k * own : (k + 1) * own]

        each(0, points // lane, tile)

    each(1, dirs - 1, lambda d: source1(d, lambda at: x[d + 1, :, at], lambda at: x[d - 1, :, at]))
    for c in rep1:
        c.wait_recv()
    source1(0, lambda at: x[1, :, at], lambda at: halo[0, :, at])
    source1(dirs - 1, lambda at: halo[1, :, at], lambda at: x[dirs - 2, :, at])
    each(1, n, lambda o: in_copy(o).start())

    half = pad + 8
    width = min(512, cells)

    def gather_in(values, params, frm, first):
        v = jnp.concatenate([values, params], axis=0)
        low = v - v.astype(jnp.bfloat16).astype(jnp.float32)
        lhs[...] = jnp.concatenate([v, low], axis=0).astype(jnp.bfloat16)

        def tile(t):
            at = pl.ds(pl.multiple_of(t * width, width), width)
            point = lax.broadcasted_iota(jnp.int32, (points, width), 0)
            hot = jnp.where(point == slot[:, at] - frm * points, 1.0, 0.0).astype(jnp.bfloat16)
            r = jnp.dot(lhs[...], hot, preferred_element_type=jnp.float32)
            r = r[:half] + r[half:]
            if first:
                acc[:, at] = r
            else:
                acc[:, at] += r

        each(0, cells // width, tile)

    gather_in(send[me], pts[...], me, True)

    def arrived(o):
        frm = lax.rem(me + n - o, n)
        par_copy(o).wait_recv()
        in_copy(o).wait_recv()
        gather_in(recv[frm], precv[frm], frm, False)

    each(1, n, arrived)

    def row_copies(rows, sem):
        last = pl.ds(cells - cols, cols)
        return (
            copy(acc.at[pl.ds(0, pad), last], rows.at[0], sem, "sub", sub_next),
            copy(acc.at[pl.ds(0, pad), pl.ds(0, cols)], rows.at[1], sem + 1, "sub", sub_prev),
        )

    def start_rows(rows, sem):
        to_next, to_prev = row_copies(rows, sem)

        @pl.when(sub < ns - 1)
        def _():
            to_next.start()

        @pl.when(sub > 0)
        def _():
            to_prev.start()

    def recv_rows(rows, sem):
        to_next, to_prev = row_copies(rows, sem)

        @pl.when(sub > 0)
        def _():
            to_next.wait_recv()

        @pl.when(sub == 0)
        def _():
            rows[0] = jnp.zeros((pad, cols), jnp.float32)

        @pl.when(sub < ns - 1)
        def _():
            to_prev.wait_recv()

        @pl.when(sub == ns - 1)
        def _():
            rows[1] = jnp.zeros((pad, cols), jnp.float32)

    def sent_rows(rows, sem):
        to_next, to_prev = row_copies(rows, sem)

        @pl.when(sub < ns - 1)
        def _():
            to_next.wait_send()

        @pl.when(sub > 0)
        def _():
            to_prev.wait_send()

    def moved(d, rows):
        at = pl.ds(pl.multiple_of(d * own, own), own)
        e = acc[at, :]
        below = jnp.concatenate([rows[0, at, :], e[:, : cells - cols]], axis=1)
        above = jnp.concatenate([e[:, cols:], rows[1, at, :]], axis=1)
        left = pltpu.roll(e, 1, 1) * marks[1:2, :]
        right = pltpu.roll(e, cells - 1, 1) * marks[2:3, :]
        speed = fown[:, classes + 1 : classes + 2]
        nux, nuy = ang[0, d] * speed, ang[1, d] * speed
        m = (
            e
            - jnp.maximum(nux, 0.0) * (e - left)
            - jnp.minimum(nux, 0.0) * (right - e)
            - jnp.maximum(nuy, 0.0) * (e - below)
            - jnp.minimum(nuy, 0.0) * (above - e)
        )
        return m * marks[0:1, :]

    start_rows(rows1, SUB1)
    rate2[...] = rate_of(fown, acc[pad + 2 : pad + 3, :], acc[pad + 3 : pad + 4, :], classes)
    recv_rows(rows1, SUB1)

    def prop1(d):
        m = moved(d, rows1)
        g[d + 1] = m
        elo[d] = m[0:1]
        ehi[d] = m[own - 1 : own]

    each(0, dirs, prop1)

    inner = pl.ds(1, dirs)
    rep2 = [
        copy(g.at[1], g.at[dirs + 1], REP2, "rep", rep_prev),
        copy(g.at[dirs], g.at[0], REP2 + 1, "rep", rep_next),
        copy(flo.at[1], flo.at[dirs + 1], REP2 + 2, "rep", rep_prev),
        copy(flo.at[dirs], flo.at[0], REP2 + 3, "rep", rep_next),
        copy(fhi.at[1], fhi.at[dirs + 1], REP2 + 4, "rep", rep_prev),
        copy(fhi.at[dirs], fhi.at[0], REP2 + 5, "rep", rep_next),
    ]
    to_upper = copy(ehi, flo.at[inner], FRQ, "cards", lax.rem(me + 1, n))
    to_lower = copy(elo, fhi.at[inner], FRQ + 1, "cards", lax.rem(me + n - 1, n))

    @pl.when(me < n - 1)
    def _():
        to_upper.start()

    @pl.when(me > 0)
    def _():
        to_lower.start()

    rep2[0].start()
    rep2[1].start()
    sent_rows(rows1, SUB1)

    @pl.when(me > 0)
    def _():
        to_upper.wait_recv()

    @pl.when(me == 0)
    def _():
        flo[inner] = jnp.zeros((dirs, 1, cells), jnp.float32)

    @pl.when(me < n - 1)
    def _():
        to_lower.wait_recv()

    @pl.when(me == n - 1)
    def _():
        fhi[inner] = jnp.zeros((dirs, 1, cells), jnp.float32)

    for c in rep2[2:]:
        c.start()

    span = min(1024, cells)

    def source2(d):
        def tile(t):
            at = pl.ds(pl.multiple_of(t * span, span), span)
            row = lax.broadcasted_iota(jnp.int32, (own, span), 0)

            def up(i):
                edge = jnp.broadcast_to(fhi[i, :, at], (own, span))
                if own == 1:
                    return edge
                return jnp.where(row == own - 1, edge, pltpu.roll(g[i, :, at], own - 1, 0))

            def down(i):
                edge = jnp.broadcast_to(flo[i, :, at], (own, span))
                if own == 1:
                    return edge
                return jnp.where(row == 0, edge, pltpu.roll(g[i, :, at], 1, 0))

            e = g[d + 1, :, at]
            a, b = acc[pad : pad + 1, at], acc[pad + 1 : pad + 2, at]
            beta = jnp.maximum(ang[0, d] * a + ang[1, d] * b, 0.0)
            grow = jnp.exp(beta * fown[:, classes : classes + 1] - rate2[:, at])
            acc[pl.ds(pl.multiple_of(d * own, own), own), at] = e * grow + nonlinear(
                e, up(d + 2), down(d), up(d), down(d + 2)
            )

        each(0, cells // span, tile)

    each(1, dirs - 1, source2)
    for c in rep2:
        c.wait_recv()
    source2(0)
    source2(dirs - 1)

    start_rows(rows2, SUB2)
    recv_rows(rows2, SUB2)

    def prop2(d):
        mv[pl.ds(pl.multiple_of(d * own, own), own), :] = moved(d, rows2)

    each(0, dirs, prop2)

    block = min(512, cells)

    def split(t):
        at = pl.ds(pl.multiple_of(t * block, block), block)
        v = mv[:, at]
        low = v - v.astype(jnp.bfloat16).astype(jnp.float32)
        lhs2[:, at] = jnp.concatenate([v, low], axis=0).astype(jnp.bfloat16)

    each(0, cells // block, split)
    tall = min(256, points)

    def gather_out(to, dst):
        def tile(t):
            base = to * points + t * tall
            point = lax.broadcasted_iota(jnp.int32, (tall, cells), 0)
            hot = jnp.where(point == slot[...] - base, 1.0, 0.0).astype(jnp.bfloat16)
            r = lax.dot_general(
                lhs2[...], hot, (((1,), (1,)), ((), ())), preferred_element_type=jnp.float32
            )
            dst[to, :, pl.ds(pl.multiple_of(t * tall, tall), tall)] = r[:pad] + r[pad:]

        each(0, points // tall, tile)

    def leave(o):
        gather_out(lax.rem(me + o, n), sback)
        out_copy(o).start()

    each(1, n, leave)
    gather_out(me, rback)

    def place(frm):
        for d in range(dirs):
            out[d, pl.ds(pl.multiple_of(frm * own, own), own), :] = rback[
                frm, d * own : (d + 1) * own, :
            ]

    place(me)

    def back(o):
        out_copy(o).wait_recv()
        place(lax.rem(me + n - o, n))

    each(1, n, back)

    for c in rep1 + rep2:
        c.wait_send()

    @pl.when(me < n - 1)
    def _():
        to_upper.wait_send()

    @pl.when(me > 0)
    def _():
        to_lower.wait_send()

    sent_rows(rows2, SUB2)

    def gone(o):
        par_copy(o).wait_send()
        in_copy(o).wait_send()
        out_copy(o).wait_send()

    each(1, n, gone)


def shards(spectra, deal_slot, sea_mask, ice_class, brine, wind_rate, wind_dir, ice_table):
    dirs, freqs, _, points = spectra.shape
    n = lax.axis_size("cards")
    me = lax.axis_index("cards")
    ns = lax.axis_size("sub")
    nrep = lax.axis_size("rep")
    rep = lax.axis_index("rep")
    own = freqs // n
    rows, cols = sea_mask.shape
    cells = rows * cols
    classes = ice_table.shape[0]
    comp = dirs * own
    pad = -(-comp // 8) * 8

    theta = 2.0 * jnp.pi * jnp.arange(dirs * nrep, dtype=jnp.float32) / (dirs * nrep)
    theta = lax.dynamic_slice_in_dim(theta, rep * dirs, dirs, 0)
    ang = jnp.stack([jnp.cos(theta), jnp.sin(theta)])
    freq = F0 * GROWTH ** jnp.arange(freqs, dtype=jnp.float32)
    fall = jnp.concatenate(
        [ice_table.T, (freq / freq[-1])[:, None], (COURANT * (freq[0] / freq))[:, None]], axis=1
    )
    fown = lax.dynamic_slice_in_dim(fall, me * own, own, 0)
    wave = wind_rate[0]
    point_rows = [
        wave * jnp.cos(wind_dir[0]),
        wave * jnp.sin(wind_dir[0]),
        ice_class[0].astype(jnp.float32),
        jnp.sqrt(brine[0] / 0.1),
    ]
    pts = jnp.stack(point_rows + [jnp.zeros_like(wave)] * 4)
    col = lax.broadcasted_iota(jnp.int32, (rows, cols), 1).reshape(-1)
    marks = jnp.stack(
        [
            sea_mask.reshape(-1).astype(jnp.float32),
            (col != 0).astype(jnp.float32),
            (col != cols - 1).astype(jnp.float32),
        ]
    )
    f32 = jnp.float32
    vmem = pltpu.VMEM
    count = 14 + 3 * n
    sizes = (dirs, freqs, points, n, own, ns, nrep, classes, cols)
    spec = pl.BlockSpec(memory_space=pltpu.VMEM)
    result = pl.pallas_call(
        functools.partial(kernel, sizes),
        out_shape=jax.ShapeDtypeStruct((dirs, freqs, points), f32),
        in_specs=[spec] * 4 + [pl.BlockSpec(memory_space=pltpu.SMEM)] + [spec] * 2,
        out_specs=spec,
        scratch_shapes=[
            vmem((2, freqs, points), f32),
            vmem((n, pad, points), f32),
            vmem((n, pad, points), f32),
            vmem((n, 8, points), f32),
            vmem((2 * (pad + 8), points), jnp.bfloat16),
            vmem((pad + 8, cells), f32),
            vmem((dirs + 2, own, cells), f32),
            vmem((dirs + 2, 1, cells), f32),
            vmem((dirs + 2, 1, cells), f32),
            vmem((dirs, 1, cells), f32),
            vmem((dirs, 1, cells), f32),
            vmem((2, pad, cols), f32),
            vmem((2, pad, cols), f32),
            vmem((freqs, points), f32),
            vmem((own, cells), f32),
            vmem((pad, cells), f32),
            vmem((2 * pad, cells), jnp.bfloat16),
            vmem((n, pad, points), f32),
            vmem((n, pad, points), f32),
            pltpu.SemaphoreType.DMA((count,)),
            pltpu.SemaphoreType.DMA((count,)),
        ],
        compiler_params=pltpu.CompilerParams(
            collective_id=0, has_side_effects=True, vmem_limit_bytes=56 * 2**20
        ),
    )(spectra.reshape(dirs, freqs, points), deal_slot, marks, pts, ang, fall, fown)
    return result[:, :, None, :]


def solution(mesh):
    placed = (
        P("rep", None, "sub", ("members", "cards")),
        P("sub", "members"),
        P("sub", "members"),
        P("sub", ("members", "cards")),
        P("sub", ("members", "cards")),
        P("sub", ("members", "cards")),
        P("sub", ("members", "cards")),
        P(),
    )
    return jax.shard_map(
        shards,
        mesh=mesh,
        in_specs=placed,
        out_specs=P("rep", None, "sub", ("members", "cards")),
        check_vma=False,
    )
```

```python
import functools

import jax
import jax.numpy as jnp
import numpy as np
from jax import lax
from jax.experimental import pallas as pl
from jax.experimental.pallas import tpu as pltpu
from jax.sharding import PartitionSpec as P

F0 = 0.035
GROWTH = 1.1
CNL = 0.25
COURANT = 0.6
MESH = pl.DeviceIdType.MESH


def nonlinear(energy, pone, mone, ptwo, mtwo):
    return CNL * (
        energy * energy * (pone + mone + ptwo + mtwo) - 2.0 * energy * (pone * mone + ptwo * mtwo)
    )


def rate_of(cols, classes, root, class_count):
    rate = jnp.zeros((cols.shape[0], classes.shape[1]), jnp.float32)
    for k in range(class_count):
        rate = jnp.where(jnp.abs(classes - k) < 0.5, cols[:, k : k + 1], rate)
    return rate * root


def kernel(
    sizes, x, slot, sea, ice_class, brine, wind_rate, wind_dir, ang_all, fall, out,
    marks, pts, ang, fown, halo, send, recv, precv, lhs, acc, g, flo, fhi, elo, ehi, rows1, rows2,
    rate1, rate2, mv, lhs2, sback, rback, ssem, rsem,
):
    dirs, freqs, points, n, own, ns, nrep, classes, grid_rows, cols = sizes
    cells = n * points
    comp = dirs * own
    pad = send.shape[1]
    me = lax.axis_index("cards")
    sub = lax.axis_index("sub")
    rep = lax.axis_index("rep")
    rep_next, rep_prev = lax.rem(rep + 1, nrep), lax.rem(rep + nrep - 1, nrep)
    sub_next, sub_prev = lax.rem(sub + 1, ns), lax.rem(sub + ns - 1, ns)

    barrier = pltpu.get_barrier_semaphore()

    def greet(o, carry):
        pl.semaphore_signal(
            barrier, inc=1, device_id={"cards": lax.rem(me + o, n)}, device_id_type=MESH
        )
        return carry

    lax.fori_loop(1, n, greet, 0)
    for name, other in (("rep", rep_next), ("rep", rep_prev), ("sub", sub_next), ("sub", sub_prev)):
        pl.semaphore_signal(barrier, inc=1, device_id={name: other}, device_id_type=MESH)
    pl.semaphore_wait(barrier, n - 1 + 4)

    def copy(src, dst, sem, name, other):
        return pltpu.make_async_remote_copy(
            src_ref=src, dst_ref=dst, send_sem=ssem.at[sem], recv_sem=rsem.at[sem],
            device_id={name: other}, device_id_type=MESH,
        )

    REP1, SUB1, SUB2, FRQ, REP2, PAR = 0, 2, 4, 6, 14, 20
    AIN = PAR + n
    AOUT = AIN + 2 * n
    tall = min(256, points)
    tiles = points // tall
    cut = (dirs // 2) * own
    cuts = ((0, cut), (cut, pad)) if cut % 8 == 0 else ((0, pad),)

    rep1 = [
        copy(x.at[0], halo.at[1], REP1, "rep", rep_prev),
        copy(x.at[dirs - 1], halo.at[0], REP1 + 1, "rep", rep_next),
    ]
    for c in rep1:
        c.start()

    def par_copy(o):
        return copy(pts, precv.at[me], PAR + o, "cards", lax.rem(me + o, n))

    def in_copy(o, part):
        to = lax.rem(me + o, n)
        first, last = cuts[part]
        at = pl.ds(first, last - first)
        return copy(send.at[to, at], recv.at[me, at], AIN + 2 * o + part, "cards", to)

    def out_copy(o, t):
        to = lax.rem(me + o, n)
        at = pl.ds(pl.multiple_of(t * tall, tall), tall)
        return copy(
            sback.at[to, :, at], rback.at[me, :, at], AOUT + o * tiles + t, "cards", to
        )

    def each(first, last, body):
        def step(i, carry):
            body(i)
            return carry

        lax.fori_loop(first, last, step, 0)

    wave = wind_rate[...]
    pts[0:1, :] = wave * jnp.cos(wind_dir[...])
    pts[1:2, :] = wave * jnp.sin(wind_dir[...])
    pts[2:3, :] = ice_class[...].astype(jnp.float32)
    pts[3:4, :] = jnp.sqrt(brine[...] / 0.1)
    pts[4:8, :] = jnp.zeros((4, points), jnp.float32)
    each(1, n, lambda o: par_copy(o).start())

    def angle(d):
        ang[0, d] = ang_all[0, rep * dirs + d]
        ang[1, d] = ang_all[1, rep * dirs + d]

    each(0, dirs, angle)
    fown[...] = fall[pl.ds(pl.multiple_of(me * own, own), own), :]
    col = lax.broadcasted_iota(jnp.int32, (1, cols), 1)
    for r in range(grid_rows):
        at = slice(r * cols, (r + 1) * cols)
        marks[0:1, at] = sea[r : r + 1, :].astype(jnp.float32)
        marks[1:2, at] = jnp.where(col == 0, 0.0, 1.0)
        marks[2:3, at] = jnp.where(col == cols - 1, 0.0, 1.0)

    rate1[...] = rate_of(fall, pts[2:3, :], pts[3:4, :], classes)
    lane = min(256, points)

    def source1(d, plus, minus):
        def tile(t):
            at = pl.ds(pl.multiple_of(t * lane, lane), lane)
            row = lax.broadcasted_iota(jnp.int32, (freqs, lane), 0)

            def up(v):
                return jnp.where(row == freqs - 1, 0.0, pltpu.roll(v, freqs - 1, 0))

            def down(v):
                return jnp.where(row == 0, 0.0, pltpu.roll(v, 1, 0))

            e, p, m = x[d, :, 0, at], plus(at), minus(at)
            beta = jnp.maximum(ang[0, d] * pts[0:1, at] + ang[1, d] * pts[1:2, at], 0.0)
            grow = jnp.exp(beta * fall[:, classes : classes + 1] - rate1[:, at])
            s = e * grow + nonlinear(e, up(p), down(m), up(m), down(p))
            for k in range(n):
                send[k, pl.ds(pl.multiple_of(d * own, own), own), at] = s[k * own : (k + 1) * own]

        each(0, points // lane, tile)

    def middle1(d):
        source1(d, lambda at: x[d + 1, :, 0, at], lambda at: x[d - 1, :, 0, at])

    each(1, dirs // 2, middle1)
    for c in rep1:
        c.wait_recv()
    source1(0, lambda at: x[1, :, 0, at], lambda at: halo[0, :, 0, at])
    if len(cuts) == 2:
        each(1, n, lambda o: in_copy(o, 0).start())
    each(dirs // 2, dirs - 1, middle1)
    source1(dirs - 1, lambda at: halo[1, :, 0, at], lambda at: x[dirs - 2, :, 0, at])
    each(1, n, lambda o: in_copy(o, len(cuts) - 1).start())

    half = pad + 8
    width = min(512, cells)

    count = cells // width

    def gather_in(values, params, frm, first, between=None):
        v = jnp.concatenate([values, params], axis=0)
        low = v - v.astype(jnp.bfloat16).astype(jnp.float32)
        lhs[...] = jnp.concatenate([v, low], axis=0).astype(jnp.bfloat16)

        def tile(t):
            at = pl.ds(pl.multiple_of(t * width, width), width)
            point = lax.broadcasted_iota(jnp.int32, (points, width), 0)
            hot = jnp.where(point == slot[:, at] - frm * points, 1.0, 0.0).astype(jnp.bfloat16)
            r = jnp.dot(lhs[...], hot, preferred_element_type=jnp.float32)
            r = r[:half] + r[half:]
            if first:
                acc[:, at] = r
            else:
                acc[:, at] += r

        tile(0)
        if count > 1:
            tile(count - 1)
        if between is not None:
            between()
        each(1, count - 1, tile)

    gather_in(send[me], pts[...], me, True)

    def row_copies(rows, sem):
        last = pl.ds(cells - cols, cols)
        return (
            copy(acc.at[pl.ds(0, pad), last], rows.at[0], sem, "sub", sub_next),
            copy(acc.at[pl.ds(0, pad), pl.ds(0, cols)], rows.at[1], sem + 1, "sub", sub_prev),
        )

    def start_rows(rows, sem):
        to_next, to_prev = row_copies(rows, sem)

        @pl.when(sub < ns - 1)
        def _():
            to_next.start()

        @pl.when(sub > 0)
        def _():
            to_prev.start()

    def recv_rows(rows, sem):
        to_next, to_prev = row_copies(rows, sem)

        @pl.when(sub > 0)
        def _():
            to_next.wait_recv()

        @pl.when(sub == 0)
        def _():
            rows[0] = jnp.zeros((pad, cols), jnp.float32)

        @pl.when(sub < ns - 1)
        def _():
            to_prev.wait_recv()

        @pl.when(sub == ns - 1)
        def _():
            rows[1] = jnp.zeros((pad, cols), jnp.float32)

    def sent_rows(rows, sem):
        to_next, to_prev = row_copies(rows, sem)

        @pl.when(sub < ns - 1)
        def _():
            to_next.wait_send()

        @pl.when(sub > 0)
        def _():
            to_prev.wait_send()

    def moved(d, rows):
        at = pl.ds(pl.multiple_of(d * own, own), own)
        e = acc[at, :]
        below = jnp.concatenate([rows[0, at, :], e[:, : cells - cols]], axis=1)
        above = jnp.concatenate([e[:, cols:], rows[1, at, :]], axis=1)
        left = pltpu.roll(e, 1, 1) * marks[1:2, :]
        right = pltpu.roll(e, cells - 1, 1) * marks[2:3, :]
        speed = fown[:, classes + 1 : classes + 2]
        nux, nuy = ang[0, d] * speed, ang[1, d] * speed
        m = (
            e
            - jnp.maximum(nux, 0.0) * (e - left)
            - jnp.minimum(nux, 0.0) * (right - e)
            - jnp.maximum(nuy, 0.0) * (e - below)
            - jnp.minimum(nuy, 0.0) * (above - e)
        )
        return m * marks[0:1, :]

    def arrived(o, between=None):
        frm = lax.rem(me + n - o, n)
        par_copy(o).wait_recv()
        for part in range(len(cuts)):
            in_copy(o, part).wait_recv()
        gather_in(recv[frm], precv[frm], frm, False, between)

    each(1, n - 1, arrived)
    arrived(n - 1, lambda: start_rows(rows1, SUB1))

    rate2[...] = rate_of(fown, acc[pad + 2 : pad + 3, :], acc[pad + 3 : pad + 4, :], classes)
    recv_rows(rows1, SUB1)

    def prop1(d):
        m = moved(d, rows1)
        g[d + 1] = m
        elo[d] = m[0:1]
        ehi[d] = m[own - 1 : own]

    prop1(0)
    prop1(dirs - 1)

    inner = pl.ds(1, dirs)
    rep2 = [
        copy(g.at[1], g.at[dirs + 1], REP2, "rep", rep_prev),
        copy(g.at[dirs], g.at[0], REP2 + 1, "rep", rep_next),
        copy(flo.at[1], flo.at[dirs + 1], REP2 + 2, "rep", rep_prev),
        copy(flo.at[dirs], flo.at[0], REP2 + 3, "rep", rep_next),
        copy(fhi.at[1], fhi.at[dirs + 1], REP2 + 4, "rep", rep_prev),
        copy(fhi.at[dirs], fhi.at[0], REP2 + 5, "rep", rep_next),
    ]
    rep2[0].start()
    rep2[1].start()
    upper, lower = lax.rem(me + 1, n), lax.rem(me + n - 1, n)
    half_dirs = dirs // 2
    groups = ((0, 1), (dirs - 1, 1), (1, half_dirs - 1), (half_dirs, dirs - 1 - half_dirs))
    to_upper, to_lower = [], []
    for i, (first, size) in enumerate(groups):
        src, dst = pl.ds(first, size), pl.ds(first + 1, size)
        to_upper.append(copy(ehi.at[src], flo.at[dst], FRQ + 2 * i, "cards", upper))
        to_lower.append(copy(elo.at[src], fhi.at[dst], FRQ + 2 * i + 1, "cards", lower))

    def start_edges(chosen):
        @pl.when(me < n - 1)
        def _():
            for i in chosen:
                to_upper[i].start()

        @pl.when(me > 0)
        def _():
            for i in chosen:
                to_lower[i].start()

    def recv_edges(chosen):
        @pl.when(me > 0)
        def _():
            for i in chosen:
                to_upper[i].wait_recv()

        @pl.when(me < n - 1)
        def _():
            for i in chosen:
                to_lower[i].wait_recv()

    @pl.when(me == 0)
    def _():
        flo[inner] = jnp.zeros((dirs, 1, cells), jnp.float32)

    @pl.when(me == n - 1)
    def _():
        fhi[inner] = jnp.zeros((dirs, 1, cells), jnp.float32)

    start_edges((0, 1))
    each(1, half_dirs, prop1)
    start_edges((2,))
    recv_edges((0, 1))
    for c in rep2[2:]:
        c.start()
    each(half_dirs, dirs - 1, prop1)
    start_edges((3,))
    sent_rows(rows1, SUB1)

    span = min(1024, cells)

    spans = cells // span

    def source2(t):
        def tile(d):
            at = pl.ds(pl.multiple_of(t * span, span), span)
            row = lax.broadcasted_iota(jnp.int32, (own, span), 0)

            def up(i):
                edge = jnp.broadcast_to(fhi[i, :, at], (own, span))
                if own == 1:
                    return edge
                return jnp.where(row == own - 1, edge, pltpu.roll(g[i, :, at], own - 1, 0))

            def down(i):
                edge = jnp.broadcast_to(flo[i, :, at], (own, span))
                if own == 1:
                    return edge
                return jnp.where(row == 0, edge, pltpu.roll(g[i, :, at], 1, 0))

            e = g[d + 1, :, at]
            a, b = acc[pad : pad + 1, at], acc[pad + 1 : pad + 2, at]
            beta = jnp.maximum(ang[0, d] * a + ang[1, d] * b, 0.0)
            grow = jnp.exp(beta * fown[:, classes : classes + 1] - rate2[:, at])
            acc[pl.ds(pl.multiple_of(d * own, own), own), at] = e * grow + nonlinear(
                e, up(d + 2), down(d), up(d), down(d + 2)
            )

        each(0, dirs, tile)

    for c in rep2:
        c.wait_recv()
    recv_edges((2, 3))
    source2(0)
    if spans > 1:
        source2(spans - 1)

    start_rows(rows2, SUB2)
    each(1, spans - 1, source2)
    recv_rows(rows2, SUB2)

    def prop2(d):
        mv[pl.ds(pl.multiple_of(d * own, own), own), :] = moved(d, rows2)

    each(0, dirs, prop2)

    block = min(512, cells)

    def split(t):
        at = pl.ds(pl.multiple_of(t * block, block), block)
        v = mv[:, at]
        low = v - v.astype(jnp.bfloat16).astype(jnp.float32)
        lhs2[:, at] = jnp.concatenate([v, low], axis=0).astype(jnp.bfloat16)

    each(0, cells // block, split)
    def gather_out(to, t, dst):
        base = to * points + t * tall
        point = lax.broadcasted_iota(jnp.int32, (tall, cells), 0)
        hot = jnp.where(point == slot[...] - base, 1.0, 0.0).astype(jnp.bfloat16)
        r = lax.dot_general(
            lhs2[...], hot, (((1,), (1,)), ((), ())), preferred_element_type=jnp.float32
        )
        dst[to, :, pl.ds(pl.multiple_of(t * tall, tall), tall)] = r[:pad] + r[pad:]

    def leave(i):
        t, o = i // (n - 1), lax.rem(i, n - 1) + 1
        gather_out(lax.rem(me + o, n), t, sback)
        out_copy(o, t).start()

    each(0, tiles * (n - 1), leave)
    each(0, tiles, lambda t: gather_out(me, t, rback))

    def place(frm):
        for d in range(dirs):
            out[d, pl.ds(pl.multiple_of(frm * own, own), own), :] = rback[
                frm, d * own : (d + 1) * own, :
            ]

    place(me)

    def back(o):
        each(0, tiles, lambda t: out_copy(o, t).wait_recv())
        place(lax.rem(me + n - o, n))

    each(1, n, back)

    for c in rep1 + rep2:
        c.wait_send()

    @pl.when(me < n - 1)
    def _():
        for c in to_upper:
            c.wait_send()

    @pl.when(me > 0)
    def _():
        for c in to_lower:
            c.wait_send()

    sent_rows(rows2, SUB2)

    def gone(o):
        par_copy(o).wait_send()
        for part in range(len(cuts)):
            in_copy(o, part).wait_send()
        each(0, tiles, lambda t: out_copy(o, t).wait_send())

    each(1, n, gone)


def shards(spectra, deal_slot, sea_mask, ice_class, brine, wind_rate, wind_dir, ice_table):
    dirs, freqs, _, points = spectra.shape
    n = lax.axis_size("cards")
    ns = lax.axis_size("sub")
    nrep = lax.axis_size("rep")
    own = freqs // n
    rows, cols = sea_mask.shape
    cells = rows * cols
    classes = ice_table.shape[0]
    comp = dirs * own
    pad = -(-comp // 8) * 8

    theta = 2.0 * np.pi * np.arange(dirs * nrep) / (dirs * nrep)
    ang = jnp.asarray(np.stack([np.cos(theta), np.sin(theta)]), jnp.float32)
    freq = F0 * GROWTH ** np.arange(freqs)
    shape = np.stack([freq / freq[-1], COURANT * (freq[0] / freq)], axis=1)
    fall = jnp.concatenate([ice_table.T, jnp.asarray(shape, jnp.float32)], axis=1)
    f32 = jnp.float32
    vmem = pltpu.VMEM
    count = 20 + 3 * n + n * (points // min(256, points))
    sizes = (dirs, freqs, points, n, own, ns, nrep, classes, rows, cols)
    spec = pl.BlockSpec(memory_space=pltpu.VMEM)
    result = pl.pallas_call(
        functools.partial(kernel, sizes),
        out_shape=jax.ShapeDtypeStruct((dirs, freqs, points), f32),
        in_specs=[spec] * 7 + [pl.BlockSpec(memory_space=pltpu.SMEM), spec],
        out_specs=spec,
        scratch_shapes=[
            vmem((3, cells), f32),
            vmem((8, points), f32),
            pltpu.SMEM((2, dirs), f32),
            vmem((own, classes + 2), f32),
            vmem((2, freqs, 1, points), f32),
            vmem((n, pad, points), f32),
            vmem((n, pad, points), f32),
            vmem((n, 8, points), f32),
            vmem((2 * (pad + 8), points), jnp.bfloat16),
            vmem((pad + 8, cells), f32),
            vmem((dirs + 2, own, cells), f32),
            vmem((dirs + 2, 1, cells), f32),
            vmem((dirs + 2, 1, cells), f32),
            vmem((dirs, 1, cells), f32),
            vmem((dirs, 1, cells), f32),
            vmem((2, pad, cols), f32),
            vmem((2, pad, cols), f32),
            vmem((freqs, points), f32),
            vmem((own, cells), f32),
            vmem((pad, cells), f32),
            vmem((2 * pad, cells), jnp.bfloat16),
            vmem((n, pad, points), f32),
            vmem((n, pad, points), f32),
            pltpu.SemaphoreType.DMA((count,)),
            pltpu.SemaphoreType.DMA((count,)),
        ],
        compiler_params=pltpu.CompilerParams(
            collective_id=0, has_side_effects=True, vmem_limit_bytes=56 * 2**20
        ),
    )(spectra, deal_slot, sea_mask, ice_class, brine, wind_rate, wind_dir, ang, fall)
    return result[:, :, None, :]


def solution(mesh):
    placed = (
        P("rep", None, "sub", ("members", "cards")),
        P("sub", "members"),
        P("sub", "members"),
        P("sub", ("members", "cards")),
        P("sub", ("members", "cards")),
        P("sub", ("members", "cards")),
        P("sub", ("members", "cards")),
        P(),
    )
    return jax.shard_map(
        shards,
        mesh=mesh,
        in_specs=placed,
        out_specs=P("rep", None, "sub", ("members", "cards")),
        check_vma=False,
    )
```

```python
import functools

import jax
import jax.numpy as jnp
import numpy as np
from jax import lax
from jax.experimental import pallas as pl
from jax.experimental.pallas import tpu as pltpu
from jax.sharding import PartitionSpec as P

F0 = 0.035
GROWTH = 1.1
CNL = 0.25
COURANT = 0.6
MESH = pl.DeviceIdType.MESH


def nonlinear(energy, pone, mone, ptwo, mtwo):
    return CNL * (
        energy * energy * (pone + mone + ptwo + mtwo) - 2.0 * energy * (pone * mone + ptwo * mtwo)
    )


def rate_of(cols, classes, root, class_count):
    rate = jnp.zeros((cols.shape[0], classes.shape[1]), jnp.float32)
    for k in range(class_count):
        rate = jnp.where(jnp.abs(classes - k) < 0.5, cols[:, k : k + 1], rate)
    return rate * root


def kernel(
    sizes, x, slot, sea, ice_class, brine, wind_rate, wind_dir, ang_all, fall, out,
    marks, pts, ang, fown, halo, send, recv, precv, lhs, acc, g, flo, fhi, elo, ehi, rows1, rows2,
    rate1, rate2, mv, lhs2, sback, rback, ssem, rsem,
):
    dirs, freqs, points, n, own, ns, nrep, classes, grid_rows, cols = sizes
    cells = n * points
    comp = dirs * own
    pad = send.shape[1]
    me = lax.axis_index("cards")
    sub = lax.axis_index("sub")
    rep = lax.axis_index("rep")
    rep_next, rep_prev = lax.rem(rep + 1, nrep), lax.rem(rep + nrep - 1, nrep)
    sub_next, sub_prev = lax.rem(sub + 1, ns), lax.rem(sub + ns - 1, ns)

    barrier = pltpu.get_barrier_semaphore()

    def greet(o, carry):
        pl.semaphore_signal(
            barrier, inc=1, device_id={"cards": lax.rem(me + o, n)}, device_id_type=MESH
        )
        return carry

    lax.fori_loop(1, n, greet, 0)
    for name, other in (("rep", rep_next), ("rep", rep_prev), ("sub", sub_next), ("sub", sub_prev)):
        pl.semaphore_signal(barrier, inc=1, device_id={name: other}, device_id_type=MESH)
    pl.semaphore_wait(barrier, n - 1 + 4)

    def copy(src, dst, sem, name, other):
        return pltpu.make_async_remote_copy(
            src_ref=src, dst_ref=dst, send_sem=ssem.at[sem], recv_sem=rsem.at[sem],
            device_id={name: other}, device_id_type=MESH,
        )

    REP1, SUB1, SUB2, FRQ, REP2, PAR = 0, 2, 4, 6, 14, 20
    AIN = PAR + n
    AOUT = AIN + 2 * n
    tall = min(256, points)
    tiles = points // tall
    cut = (dirs // 2) * own
    cuts = ((0, cut), (cut, pad)) if cut % 8 == 0 else ((0, pad),)

    rep1 = [
        copy(x.at[0], halo.at[1], REP1, "rep", rep_prev),
        copy(x.at[dirs - 1], halo.at[0], REP1 + 1, "rep", rep_next),
    ]
    for c in rep1:
        c.start()

    def par_copy(o):
        return copy(pts, precv.at[me], PAR + o, "cards", lax.rem(me + o, n))

    def in_copy(o, part):
        to = lax.rem(me + o, n)
        first, last = cuts[part]
        at = pl.ds(first, last - first)
        return copy(send.at[to, at], recv.at[me, at], AIN + 2 * o + part, "cards", to)

    def out_copy(o, t):
        to = lax.rem(me + o, n)
        at = pl.ds(pl.multiple_of(t * tall, tall), tall)
        return copy(
            sback.at[to, :, at], rback.at[me, :, at], AOUT + o * tiles + t, "cards", to
        )

    def each(first, last, body):
        def step(i, carry):
            body(i)
            return carry

        lax.fori_loop(first, last, step, 0)

    wave = wind_rate[...]
    pts[0:1, :] = wave * jnp.cos(wind_dir[...])
    pts[1:2, :] = wave * jnp.sin(wind_dir[...])
    pts[2:3, :] = ice_class[...].astype(jnp.float32)
    pts[3:4, :] = jnp.sqrt(brine[...] / 0.1)
    pts[4:8, :] = jnp.zeros((4, points), jnp.float32)
    each(1, n, lambda o: par_copy(o).start())

    def angle(d):
        ang[0, d] = ang_all[0, rep * dirs + d]
        ang[1, d] = ang_all[1, rep * dirs + d]

    each(0, dirs, angle)
    fown[...] = fall[pl.ds(pl.multiple_of(me * own, own), own), :]
    col = lax.broadcasted_iota(jnp.int32, (1, cols), 1)
    for r in range(grid_rows):
        at = slice(r * cols, (r + 1) * cols)
        marks[0:1, at] = sea[r : r + 1, :].astype(jnp.float32)
        marks[1:2, at] = jnp.where(col == 0, 0.0, 1.0)
        marks[2:3, at] = jnp.where(col == cols - 1, 0.0, 1.0)

    rate1[...] = rate_of(fall, pts[2:3, :], pts[3:4, :], classes)
    lane = min(256, points)

    def source1(d, plus, minus):
        def tile(t):
            at = pl.ds(pl.multiple_of(t * lane, lane), lane)
            row = lax.broadcasted_iota(jnp.int32, (freqs, lane), 0)

            def up(v):
                return jnp.where(row == freqs - 1, 0.0, pltpu.roll(v, freqs - 1, 0))

            def down(v):
                return jnp.where(row == 0, 0.0, pltpu.roll(v, 1, 0))

            e, p, m = x[d, :, 0, at], plus(at), minus(at)
            beta = jnp.maximum(ang[0, d] * pts[0:1, at] + ang[1, d] * pts[1:2, at], 0.0)
            grow = jnp.exp(beta * fall[:, classes : classes + 1] - rate1[:, at])
            s = e * grow + nonlinear(e, up(p), down(m), up(m), down(p))
            for k in range(n):
                send[k, pl.ds(pl.multiple_of(d * own, own), own), at] = s[k * own : (k + 1) * own]

        each(0, points // lane, tile)

    def middle1(d):
        source1(d, lambda at: x[d + 1, :, 0, at], lambda at: x[d - 1, :, 0, at])

    each(1, dirs // 2, middle1)
    for c in rep1:
        c.wait_recv()
    source1(0, lambda at: x[1, :, 0, at], lambda at: halo[0, :, 0, at])
    if len(cuts) == 2:
        each(1, n, lambda o: in_copy(o, 0).start())
    each(dirs // 2, dirs - 1, middle1)
    source1(dirs - 1, lambda at: halo[1, :, 0, at], lambda at: x[dirs - 2, :, 0, at])
    each(1, n, lambda o: in_copy(o, len(cuts) - 1).start())

    width = min(512, cells)

    count = cells // width

    def gather_in(frm, part, source, params, first, between=None):
        low_row, high_row = cuts[part]
        size = high_row - low_row
        at_rows = pl.ds(low_row, size)
        v = source[frm, at_rows, :]
        if part == 0:
            v = jnp.concatenate([v, params], axis=0)
        m = v.shape[0]
        low = v - v.astype(jnp.bfloat16).astype(jnp.float32)
        two = lhs.at[pl.ds(0, 2 * m)]
        two[...] = jnp.concatenate([v, low], axis=0).astype(jnp.bfloat16)

        def tile(t):
            at = pl.ds(pl.multiple_of(t * width, width), width)
            point = lax.broadcasted_iota(jnp.int32, (points, width), 0)
            hot = jnp.where(point == slot[:, at] - frm * points, 1.0, 0.0).astype(jnp.bfloat16)
            r = jnp.dot(two[...], hot, preferred_element_type=jnp.float32)
            r = r[:m] + r[m:]
            if first:
                acc[at_rows, at] = r[:size]
            else:
                acc[at_rows, at] += r[:size]
            if part == 0:
                extra = pl.ds(pad, 8)
                if first:
                    acc[extra, at] = r[size:]
                else:
                    acc[extra, at] += r[size:]

        tile(0)
        if count > 1:
            tile(count - 1)
        if between is not None:
            between()
        each(1, count - 1, tile)

    def row_copies(rows, sem):
        last = pl.ds(cells - cols, cols)
        return (
            copy(acc.at[pl.ds(0, pad), last], rows.at[0], sem, "sub", sub_next),
            copy(acc.at[pl.ds(0, pad), pl.ds(0, cols)], rows.at[1], sem + 1, "sub", sub_prev),
        )

    def start_rows(rows, sem):
        to_next, to_prev = row_copies(rows, sem)

        @pl.when(sub < ns - 1)
        def _():
            to_next.start()

        @pl.when(sub > 0)
        def _():
            to_prev.start()

    def recv_rows(rows, sem):
        to_next, to_prev = row_copies(rows, sem)

        @pl.when(sub > 0)
        def _():
            to_next.wait_recv()

        @pl.when(sub == 0)
        def _():
            rows[0] = jnp.zeros((pad, cols), jnp.float32)

        @pl.when(sub < ns - 1)
        def _():
            to_prev.wait_recv()

        @pl.when(sub == ns - 1)
        def _():
            rows[1] = jnp.zeros((pad, cols), jnp.float32)

    def sent_rows(rows, sem):
        to_next, to_prev = row_copies(rows, sem)

        @pl.when(sub < ns - 1)
        def _():
            to_next.wait_send()

        @pl.when(sub > 0)
        def _():
            to_prev.wait_send()

    def moved(d, rows):
        at = pl.ds(pl.multiple_of(d * own, own), own)
        e = acc[at, :]
        below = jnp.concatenate([rows[0, at, :], e[:, : cells - cols]], axis=1)
        above = jnp.concatenate([e[:, cols:], rows[1, at, :]], axis=1)
        left = pltpu.roll(e, 1, 1) * marks[1:2, :]
        right = pltpu.roll(e, cells - 1, 1) * marks[2:3, :]
        speed = fown[:, classes + 1 : classes + 2]
        nux, nuy = ang[0, d] * speed, ang[1, d] * speed
        m = (
            e
            - jnp.maximum(nux, 0.0) * (e - left)
            - jnp.minimum(nux, 0.0) * (right - e)
            - jnp.maximum(nuy, 0.0) * (e - below)
            - jnp.minimum(nuy, 0.0) * (above - e)
        )
        return m * marks[0:1, :]

    def arrived(o, part, between=None):
        frm = lax.rem(me + n - o, n)
        if part == 0:
            par_copy(o).wait_recv()
        in_copy(o, part).wait_recv()
        gather_in(frm, part, recv, precv[frm], False, between)

    for part in range(len(cuts)):
        gather_in(me, part, send, pts[...], True)
        if part < len(cuts) - 1:
            each(1, n, lambda o: arrived(o, part))
    each(1, n - 1, lambda o: arrived(o, len(cuts) - 1))
    arrived(n - 1, len(cuts) - 1, lambda: start_rows(rows1, SUB1))

    rate2[...] = rate_of(fown, acc[pad + 2 : pad + 3, :], acc[pad + 3 : pad + 4, :], classes)
    recv_rows(rows1, SUB1)

    def prop1(d):
        m = moved(d, rows1)
        g[d + 1] = m
        elo[d] = m[0:1]
        ehi[d] = m[own - 1 : own]

    prop1(0)
    prop1(dirs - 1)

    inner = pl.ds(1, dirs)
    rep2 = [
        copy(g.at[1], g.at[dirs + 1], REP2, "rep", rep_prev),
        copy(g.at[dirs], g.at[0], REP2 + 1, "rep", rep_next),
        copy(flo.at[1], flo.at[dirs + 1], REP2 + 2, "rep", rep_prev),
        copy(flo.at[dirs], flo.at[0], REP2 + 3, "rep", rep_next),
        copy(fhi.at[1], fhi.at[dirs + 1], REP2 + 4, "rep", rep_prev),
        copy(fhi.at[dirs], fhi.at[0], REP2 + 5, "rep", rep_next),
    ]
    rep2[0].start()
    rep2[1].start()
    upper, lower = lax.rem(me + 1, n), lax.rem(me + n - 1, n)
    half_dirs = dirs // 2
    groups = ((0, 1), (dirs - 1, 1), (1, half_dirs - 1), (half_dirs, dirs - 1 - half_dirs))
    to_upper, to_lower = [], []
    for i, (first, size) in enumerate(groups):
        src, dst = pl.ds(first, size), pl.ds(first + 1, size)
        to_upper.append(copy(ehi.at[src], flo.at[dst], FRQ + 2 * i, "cards", upper))
        to_lower.append(copy(elo.at[src], fhi.at[dst], FRQ + 2 * i + 1, "cards", lower))

    def start_edges(chosen):
        @pl.when(me < n - 1)
        def _():
            for i in chosen:
                to_upper[i].start()

        @pl.when(me > 0)
        def _():
            for i in chosen:
                to_lower[i].start()

    def recv_edges(chosen):
        @pl.when(me > 0)
        def _():
            for i in chosen:
                to_upper[i].wait_recv()

        @pl.when(me < n - 1)
        def _():
            for i in chosen:
                to_lower[i].wait_recv()

    @pl.when(me == 0)
    def _():
        flo[inner] = jnp.zeros((dirs, 1, cells), jnp.float32)

    @pl.when(me == n - 1)
    def _():
        fhi[inner] = jnp.zeros((dirs, 1, cells), jnp.float32)

    start_edges((0, 1))
    each(1, half_dirs, prop1)
    start_edges((2,))
    recv_edges((0, 1))
    for c in rep2[2:]:
        c.start()
    each(half_dirs, dirs - 1, prop1)
    start_edges((3,))
    sent_rows(rows1, SUB1)

    span = min(1024, cells)

    spans = cells // span

    def source2(t):
        def tile(d):
            at = pl.ds(pl.multiple_of(t * span, span), span)
            row = lax.broadcasted_iota(jnp.int32, (own, span), 0)

            def up(i):
                edge = jnp.broadcast_to(fhi[i, :, at], (own, span))
                if own == 1:
                    return edge
                return jnp.where(row == own - 1, edge, pltpu.roll(g[i, :, at], own - 1, 0))

            def down(i):
                edge = jnp.broadcast_to(flo[i, :, at], (own, span))
                if own == 1:
                    return edge
                return jnp.where(row == 0, edge, pltpu.roll(g[i, :, at], 1, 0))

            e = g[d + 1, :, at]
            a, b = acc[pad : pad + 1, at], acc[pad + 1 : pad + 2, at]
            beta = jnp.maximum(ang[0, d] * a + ang[1, d] * b, 0.0)
            grow = jnp.exp(beta * fown[:, classes : classes + 1] - rate2[:, at])
            acc[pl.ds(pl.multiple_of(d * own, own), own), at] = e * grow + nonlinear(
                e, up(d + 2), down(d), up(d), down(d + 2)
            )

        each(0, dirs, tile)

    for c in rep2:
        c.wait_recv()
    recv_edges((2, 3))
    source2(0)
    if spans > 1:
        source2(spans - 1)

    start_rows(rows2, SUB2)
    each(1, spans - 1, source2)
    recv_rows(rows2, SUB2)

    def prop2(d):
        mv[pl.ds(pl.multiple_of(d * own, own), own), :] = moved(d, rows2)

    each(0, dirs, prop2)

    block = min(512, cells)

    def split(t):
        at = pl.ds(pl.multiple_of(t * block, block), block)
        v = mv[:, at]
        low = v - v.astype(jnp.bfloat16).astype(jnp.float32)
        lhs2[:, at] = jnp.concatenate([v, low], axis=0).astype(jnp.bfloat16)

    each(0, cells // block, split)
    def gather_out(to, t, dst):
        base = to * points + t * tall
        point = lax.broadcasted_iota(jnp.int32, (tall, cells), 0)
        hot = jnp.where(point == slot[...] - base, 1.0, 0.0).astype(jnp.bfloat16)
        r = lax.dot_general(
            lhs2[...], hot, (((1,), (1,)), ((), ())), preferred_element_type=jnp.float32
        )
        dst[to, :, pl.ds(pl.multiple_of(t * tall, tall), tall)] = r[:pad] + r[pad:]

    def leave(i):
        t, o = i // (n - 1), lax.rem(i, n - 1) + 1
        gather_out(lax.rem(me + o, n), t, sback)
        out_copy(o, t).start()

    each(0, tiles * (n - 1), leave)
    each(0, tiles, lambda t: gather_out(me, t, rback))

    def place(frm):
        for d in range(dirs):
            out[d, pl.ds(pl.multiple_of(frm * own, own), own), :] = rback[
                frm, d * own : (d + 1) * own, :
            ]

    place(me)

    def back(o):
        each(0, tiles, lambda t: out_copy(o, t).wait_recv())
        place(lax.rem(me + n - o, n))

    each(1, n, back)

    for c in rep1 + rep2:
        c.wait_send()

    @pl.when(me < n - 1)
    def _():
        for c in to_upper:
            c.wait_send()

    @pl.when(me > 0)
    def _():
        for c in to_lower:
            c.wait_send()

    sent_rows(rows2, SUB2)

    def gone(o):
        par_copy(o).wait_send()
        for part in range(len(cuts)):
            in_copy(o, part).wait_send()
        each(0, tiles, lambda t: out_copy(o, t).wait_send())

    each(1, n, gone)


def shards(spectra, deal_slot, sea_mask, ice_class, brine, wind_rate, wind_dir, ice_table):
    dirs, freqs, _, points = spectra.shape
    n = lax.axis_size("cards")
    ns = lax.axis_size("sub")
    nrep = lax.axis_size("rep")
    own = freqs // n
    rows, cols = sea_mask.shape
    cells = rows * cols
    classes = ice_table.shape[0]
    comp = dirs * own
    pad = -(-comp // 8) * 8

    theta = 2.0 * np.pi * np.arange(dirs * nrep) / (dirs * nrep)
    ang = jnp.asarray(np.stack([np.cos(theta), np.sin(theta)]), jnp.float32)
    freq = F0 * GROWTH ** np.arange(freqs)
    shape = np.stack([freq / freq[-1], COURANT * (freq[0] / freq)], axis=1)
    fall = jnp.concatenate([ice_table.T, jnp.asarray(shape, jnp.float32)], axis=1)
    f32 = jnp.float32
    vmem = pltpu.VMEM
    count = 20 + 3 * n + n * (points // min(256, points))
    sizes = (dirs, freqs, points, n, own, ns, nrep, classes, rows, cols)
    spec = pl.BlockSpec(memory_space=pltpu.VMEM)
    result = pl.pallas_call(
        functools.partial(kernel, sizes),
        out_shape=jax.ShapeDtypeStruct((dirs, freqs, points), f32),
        in_specs=[spec] * 7 + [pl.BlockSpec(memory_space=pltpu.SMEM), spec],
        out_specs=spec,
        scratch_shapes=[
            vmem((3, cells), f32),
            vmem((8, points), f32),
            pltpu.SMEM((2, dirs), f32),
            vmem((own, classes + 2), f32),
            vmem((2, freqs, 1, points), f32),
            vmem((n, pad, points), f32),
            vmem((n, pad, points), f32),
            vmem((n, 8, points), f32),
            vmem((2 * (pad + 8), points), jnp.bfloat16),
            vmem((pad + 8, cells), f32),
            vmem((dirs + 2, own, cells), f32),
            vmem((dirs + 2, 1, cells), f32),
            vmem((dirs + 2, 1, cells), f32),
            vmem((dirs, 1, cells), f32),
            vmem((dirs, 1, cells), f32),
            vmem((2, pad, cols), f32),
            vmem((2, pad, cols), f32),
            vmem((freqs, points), f32),
            vmem((own, cells), f32),
            vmem((pad, cells), f32),
            vmem((2 * pad, cells), jnp.bfloat16),
            vmem((n, pad, points), f32),
            vmem((n, pad, points), f32),
            pltpu.SemaphoreType.DMA((count,)),
            pltpu.SemaphoreType.DMA((count,)),
        ],
        compiler_params=pltpu.CompilerParams(
            collective_id=0, has_side_effects=True, vmem_limit_bytes=56 * 2**20
        ),
    )(spectra, deal_slot, sea_mask, ice_class, brine, wind_rate, wind_dir, ang, fall)
    return result[:, :, None, :]


def solution(mesh):
    placed = (
        P("rep", None, "sub", ("members", "cards")),
        P("sub", "members"),
        P("sub", "members"),
        P("sub", ("members", "cards")),
        P("sub", ("members", "cards")),
        P("sub", ("members", "cards")),
        P("sub", ("members", "cards")),
        P(),
    )
    return jax.shard_map(
        shards,
        mesh=mesh,
        in_specs=placed,
        out_specs=P("rep", None, "sub", ("members", "cards")),
        check_vma=False,
    )
```
